128 devices in a mesh: grid: 32 (over y, x, z_lo), mode: 4 (over z_hi, core).
Axes of the slice: x: 4, y: 4, z: 4 (z_hi: 2, z_lo: 2; z = z_hi * 2 + z_lo), core: 2. Of those that a mesh axis runs over, the one named last changes fastest.
Arguments:
- held_modes: bfloat16 [224, 3, 128, 4, 128], P('mode', None, 'grid'), may hold values from -6 to 6
- new_modes: bfloat16 [32, 3, 128, 4, 128], P('mode', None, 'grid'), may hold values from -6 to 6
Outputs:
- new_third: float32 [256, 8192], P('grid', 'mode')
- held_third_new_first: float32 [256, 7168], P('grid', 'mode')
- held_third_new_second: float32 [224, 7168], P('grid', 'mode')
The draws below stay inside these ranges and needn't reach their ends.
All inputs are finite; a program needn't handle non-finite values.
Results may differ from the reference program's by a relative error of at most 0.0042.
Values may be sent and summed in bfloat16 or wider, within the bound.
A program may use at most 128 MiB of HBM per device.

```python
import math
import jax
import jax.numpy as jnp
from jax import lax

HELD = 224
NEW = 32
MODES = 256
NY = 4
NZ = 128
NX = 128


def steps_of(key, extent, split, low, largest):
    gain, own = 1.0, jax.random.fold_in(key, 6)
    for axis_at, parts in split:
        draws = jnp.exp(jax.random.uniform(jax.random.fold_in(own, axis_at), (parts,), jnp.float32, low / len(split), largest / len(split)))
        gain = gain * jnp.repeat(draws, extent[axis_at] // parts).reshape([-1 if axis == axis_at else 1 for axis in range(len(extent))])
    return gain


def noise(rng, extent, spread, bound, pieces=(), dtype=jnp.bfloat16):
    result = jax.random.normal(rng, extent, jnp.float32) * spread
    if len(pieces) > 0:
        result = steps_of(rng, extent, pieces, -0.22, 0.18) * result
    return jnp.clip(result, min=-bound, max=bound).astype(dtype)


def setup_inputs(seed: int = 0) -> dict:
    splits = jax.random.split(jax.random.key(seed), 3)
    held_modes = noise(splits[0], (HELD, 3, NX, NY, NZ), 1.0, 6.0, ((0, 4), (2, 32)))
    new_modes = noise(splits[1], (NEW, 3, NX, NY, NZ), 1.0, 6.0, ((0, 4), (2, 32)))
    return {"held_modes": held_modes, "new_modes": new_modes}


def gradients(field):
    values = field.astype(jnp.float32)
    along_x = (jnp.roll(values, -1, -3) - jnp.roll(values, 1, -3)) * 0.5
    along_y = (jnp.roll(values, -1, -2) - jnp.roll(values, 1, -2)) * 0.5
    along_z = (jnp.roll(values, -1, -1) - jnp.roll(values, 1, -1)) * 0.5
    return jnp.stack([along_x, along_y, along_z], axis=-4).astype(jnp.bfloat16)

def advect(velocity, grad_block):
    first = velocity[None, :, None, 0].astype(jnp.float32) * grad_block[:, None, :, 0].astype(jnp.float32)
    second = velocity[None, :, None, 1].astype(jnp.float32) * grad_block[:, None, :, 1].astype(jnp.float32)
    third = velocity[None, :, None, 2].astype(jnp.float32) * grad_block[:, None, :, 2].astype(jnp.float32)
    return (first + second + third).astype(jnp.bfloat16)

def reference(held_modes, new_modes):
    cell_count = NX * NY * NZ
    weighting = 1.0 / math.sqrt(NX * NY * NZ)
    every = jnp.concatenate([held_modes, new_modes], 0)
    slopes = gradients(every).reshape(MODES, 3, 3, cell_count)
    velocity = every.reshape(MODES, 3, cell_count)
    all_flat = velocity.reshape(MODES, 3 * cell_count).astype(jnp.float32)
    new_flat = all_flat[HELD:]

    def new_third_one(grad_one):
        advected = advect(velocity, grad_one[None])[0].reshape(MODES, 3 * cell_count)
        return jnp.dot(all_flat, advected.astype(jnp.float32).T, preferred_element_type=jnp.float32) * weighting
    blocks = lax.map(new_third_one, slopes[HELD:])
    new_third = blocks.transpose(1, 0, 2).reshape(MODES, NEW * MODES)

    def held_third_one(grad_one):
        adv_new = advect(velocity[HELD:], grad_one[None])[0].reshape(NEW, 3 * cell_count)
        adv_held = advect(velocity[:HELD], grad_one[None])[0].reshape(HELD, 3 * cell_count)
        onto_all = jnp.dot(all_flat, adv_new.astype(jnp.float32).T, preferred_element_type=jnp.float32) * weighting
        onto_new = jnp.dot(adv_held.astype(jnp.float32), new_flat.T, preferred_element_type=jnp.float32) * weighting
        return (onto_all, onto_new)
    onto_all, onto_new = lax.map(held_third_one, slopes[:HELD])
    held_third_new_second = onto_all[:, :HELD].transpose(1, 0, 2).reshape(HELD, HELD * NEW)
    joined = jnp.concatenate([onto_new, onto_all[:, HELD:].transpose(0, 2, 1)], axis=1)
    held_third_new_first = joined.transpose(1, 0, 2).reshape(MODES, HELD * NEW)
    return (new_third, held_third_new_first, held_third_new_second)
```

```python
import math

import jax
import jax.numpy as jnp
from jax import lax
from jax.experimental import pallas as pl
from jax.experimental.pallas import tpu as pltpu
from jax.sharding import PartitionSpec as P

MESH = pl.DeviceIdType.MESH
F32 = jnp.float32
BF16 = jnp.bfloat16
PLANES = 4
LINES = 4
LANES = 128
DEPTH = 3 * LINES * LANES
ROWS = 64
HELD = 56
NEW = 8
TOTAL = 256
NEWS = 32
GROUP = 28
HCOLS = GROUP * NEWS
ACOLS = 1024
WEIGHT = 1.0 / 256.0


def row_every(g):
    i = 8 * g
    return 64 * (i // 56) + i % 56 if i < 224 else 64 * ((i - 224) // 8) + 56


def row_held(g):
    i = 7 * g
    return 64 * (i // 56) + i % 56


def kernel(
    own, out_a, out_w, out_q,
    halo, vall, vnew, slope, left, right, acc_h, acc_a,
    f_h, s1_h, r1_h, t1_h, s2_h, r2_h, t2_h, r3_h,
    f_a, s1_a, r1_a, t1_a, s2_a, r2_a, t2_a, r3_a,
    halo_send, halo_recv, gat_send, gat_recv, own_sem,
    rs1_send, rs1_recv, rs2_send, rs2_recv, rs3_send, rs3_recv,
):
    g = lax.axis_index("grid")
    m = lax.axis_index("mode")
    py, px, pz = g // 8, (g // 2) % 4, g % 2
    core = m + 1 - 2 * (m % 2)
    far = (m + 2) % 4
    far_core = (core + 2) % 4

    def cell(y, x, z):
        return (y * 4 + x) * 2 + z

    ahead, behind = (g + 1) % 32, (g + 31) % 32
    along_x = [(cell(py, (px + d) % 4, pz), m) for d in (1, 2, 3)]
    along_y = [(cell((py + d) % 4, px, pz), m) for d in (1, 2, 3)]
    across = (cell(py, px, 1 - pz), m)

    barrier = pltpu.get_barrier_semaphore()
    greeted = [(ahead, m), (behind, m), (g, core), (g, far), across] + along_x + along_y
    for other in greeted:
        pl.semaphore_signal(barrier, inc=1, device_id=other, device_id_type=MESH)
    pl.semaphore_wait(barrier, len(greeted))

    def remote(src, dst, send, recv, device):
        return pltpu.make_async_remote_copy(
            src_ref=src, dst_ref=dst, send_sem=send, recv_sem=recv,
            device_id=device, device_id_type=MESH,
        )

    def slot(who):
        return pl.ds(pl.multiple_of(who * ROWS, ROWS), ROWS)

    to_ahead = remote(own.at[PLANES - 1], halo.at[0], halo_send.at[0], halo_recv.at[0], (ahead, m))
    to_behind = remote(own.at[0], halo.at[1], halo_send.at[1], halo_recv.at[1], (behind, m))

    def to_far(x):
        return remote(own.at[x], vall.at[x, slot(m)], gat_send.at[0, x], gat_recv.at[0, x], (g, far))

    def to_core(x):
        return remote(own.at[x], vall.at[x, slot(m)], gat_send.at[1, x], gat_recv.at[1, x], (g, core))

    def pass_on(x):
        return remote(
            vall.at[x, slot(far)], vall.at[x, slot(far)], gat_send.at[2, x], gat_recv.at[2, x], (g, core)
        )

    def keep(x):
        return pltpu.make_async_copy(own.at[x], vall.at[x, slot(m)], own_sem.at[x])

    to_ahead.start()
    to_behind.start()
    for x in range(PLANES):
        to_far(x).start()
        to_core(x).start()
        keep(x).start()

    def part(ref, index, a, y):
        return ref[index, :, (a * LINES + y) * LANES : (a * LINES + y + 1) * LANES].astype(F32)

    to_ahead.wait()
    to_behind.wait()
    for x in range(PLANES):
        for a in range(3):
            centre = [part(own, x, a, y) for y in range(LINES)]
            for y in range(LINES):
                after = part(own, x + 1, a, y) if x + 1 < PLANES else part(halo, 1, a, y)
                before = part(own, x - 1, a, y) if x > 0 else part(halo, 0, a, y)
                slope[x, a, y] = (after - before) * 0.5
                slope[x, 3 + a, y] = (centre[(y + 1) % LINES] - centre[(y - 1) % LINES]) * 0.5
                slope[x, 6 + a, y] = (
                    pltpu.roll(centre[y], LANES - 1, 1) - pltpu.roll(centre[y], 1, 1)
                ) * 0.5

    def spread(x, a, b, y, k):
        row = slope[x, b * 3 + a, y, k : k + 1, :]
        return jnp.broadcast_to(row, (16, LANES)).astype(BF16)[None]

    def lanes(a, y):
        return slice((a * LINES + y) * LANES, (a * LINES + y + 1) * LANES)

    def build_held(x, half, into):
        for y in range(LINES):
            v = [vnew[x, :, lanes(b, y)].reshape(2, 16, LANES) for b in range(3)]
            for k in range(GROUP):
                s = [[spread(x, a, b, y, half * GROUP + k) for b in range(3)] for a in range(3)]
                for c in range(3):
                    w = v[0] * s[0][c] + v[1] * s[1][c] + v[2] * s[2][c]
                    into[k * NEWS : (k + 1) * NEWS, lanes(c, y)] = w.reshape(NEWS, LANES)
                for c in range(3):
                    q = v[0] * s[c][0] + v[1] * s[c][1] + v[2] * s[c][2]
                    into[HCOLS + k * NEWS : HCOLS + (k + 1) * NEWS, lanes(c, y)] = q.reshape(NEWS, LANES)

    def build_new(x, half, into):
        for y in range(LINES):
            for k in range(4):
                s = [[spread(x, a, b, y, HELD + half * 4 + k) for b in range(3)] for a in range(3)]
                v = [vall[x, :, lanes(b, y)].reshape(16, 16, LANES) for b in range(3)]
                for c in range(3):
                    q = v[0] * s[c][0] + v[1] * s[c][1] + v[2] * s[c][2]
                    into[k * TOTAL : (k + 1) * TOTAL, lanes(c, y)] = q.reshape(TOTAL, LANES)

    def contract(x, block):
        return lax.dot_general(
            vall[x], block, (((1,), (1,)), ((), ())), preferred_element_type=F32
        )

    def arrive(x):
        to_far(x).wait_recv()
        pass_on(x).start()
        keep(x).wait()
        to_core(x).wait_recv()
        pass_on(x).wait_recv()
        for pair in range(2):
            tops = [
                vall[x, (2 * pair + e) * ROWS + 48 : (2 * pair + e) * ROWS + 64, :].astype(F32)[8:16]
                for e in range(2)
            ]
            vnew[x, pair * 16 : (pair + 1) * 16, :] = jnp.concatenate(tops, 0).astype(BF16)

    acc_h[...] = jnp.zeros_like(acc_h)
    acc_a[...] = jnp.zeros_like(acc_a)
    arrive(0)
    build_held(0, 0, left)

    def plane(x, carry):
        build_held(x, 1, right)
        acc_h[0] += contract(x, left[...])

        @pl.when(x < PLANES - 1)
        def _():
            arrive(x + 1)

        build_held(jnp.minimum(x + 1, PLANES - 1), 0, left)
        acc_h[1] += contract(x, right[...])
        return carry

    lax.fori_loop(0, PLANES, plane, 0)

    class Job:
        def __init__(self, n, bufs, width, source, maps, sinks):
            self.n, self.width, self.source, self.maps, self.sinks = n, width, source, maps, sinks
            self.f, self.s1, self.r1, self.t1, self.s2, self.r2, self.t2, self.r3 = bufs

        def first(self):
            for e in range(2):
                for p in range(4):
                    for q in range(4):
                        at = (q * 4 + p) if e == 0 else (p * 4 + q)
                        rows = [self.maps[e](2 * at + z) for z in range(2)]
                        for z in range(2):
                            self.f[e, p, q * 16 + z * 8 : q * 16 + z * 8 + 8, :] = self.source(e, rows[z])
                        self.s1[e, p, q * 16 : q * 16 + 16, :] = self.f[e, p, q * 16 : q * 16 + 16, :].astype(BF16)
            for copy in self.copies1():
                copy.start()

        def copies1(self):
            found = []
            for d in (1, 2, 3):
                for e in range(2):
                    p = ((px if e == 0 else py) + d) % 4
                    found.append(
                        remote(
                            self.s1.at[e, p], self.r1.at[e, d - 1],
                            rs1_send.at[self.n, e, d - 1], rs1_recv.at[self.n, e, d - 1],
                            (along_x if e == 0 else along_y)[d - 1],
                        )
                    )
            return found

        def second(self):
            for copy in self.copies1():
                copy.wait()
            for e in range(2):
                p = px if e == 0 else py
                t = self.f[e, p]
                for d in range(3):
                    t = t + self.r1[e, d].astype(F32)
                for q in range(4):
                    self.t1[e, q] = t[q * 16 : q * 16 + 16]
                    self.s2[e, q] = t[q * 16 : q * 16 + 16].astype(BF16)
            for copy in self.copies2():
                copy.start()

        def copies2(self):
            found = []
            for d in (1, 2, 3):
                for e in range(2):
                    q = ((py if e == 0 else px) + d) % 4
                    found.append(
                        remote(
                            self.s2.at[e, q], self.r2.at[e, d - 1],
                            rs2_send.at[self.n, e, d - 1], rs2_recv.at[self.n, e, d - 1],
                            (along_y if e == 0 else along_x)[d - 1],
                        )
                    )
            return found

        def third(self):
            for copy in self.copies2():
                copy.wait()
            for e in range(2):
                t = self.t1[e, py if e == 0 else px]
                for d in range(3):
                    t = t + self.r2[e, d].astype(F32)
                self.t2[e, 0] = t[0:8]
                self.t2[e, 1] = t[8:16]
            for copy in self.copies3():
                copy.start()

        def copies3(self):
            return [
                remote(
                    self.t2.at[e, 1 - pz], self.r3.at[e],
                    rs3_send.at[self.n, e], rs3_recv.at[self.n, e], across,
                )
                for e in range(2)
            ]

        def last(self):
            for copy in self.copies3():
                copy.wait()
            for e in range(2):
                ref, at = self.sinks[e]
                ref[:, at : at + self.width] = (self.t2[e, pz] + self.r3[e]) * WEIGHT

    def held_job(half):
        def source(e, row):
            return acc_h[half, row : row + 8, e * HCOLS : (e + 1) * HCOLS]

        bufs = [b.at[half] for b in (f_h, s1_h, r1_h, t1_h, s2_h, r2_h, t2_h, r3_h)]
        return Job(half, bufs, HCOLS, source, (row_every, row_held),
                   ((out_w, half * HCOLS), (out_q, half * HCOLS)))

    def new_job():
        def source(e, row):
            return acc_a[e, row : row + 8, :]

        return Job(2, (f_a, s1_a, r1_a, t1_a, s2_a, r2_a, t2_a, r3_a), ACOLS, source,
                   (row_every, row_every), ((out_a, 0), (out_a, ACOLS)))

    jobs = [held_job(0), held_job(1), new_job()]
    jobs[0].first()
    jobs[1].first()

    build_new(0, 0, left.at[0:ACOLS])

    def new_plane(x):
        build_new(x, 1, right.at[0:ACOLS])
        acc_a[0] += contract(x, left[0:ACOLS])
        if x + 1 < PLANES:
            build_new(x + 1, 0, left.at[0:ACOLS])
        acc_a[1] += contract(x, right[0:ACOLS])

    new_plane(0)
    new_plane(1)
    jobs[0].second()
    new_plane(2)
    jobs[1].second()
    new_plane(3)
    jobs[2].first()
    jobs[0].third()
    jobs[1].third()
    jobs[0].last()
    jobs[1].last()
    jobs[2].second()
    jobs[2].third()
    jobs[2].last()
    for x in range(PLANES):
        to_far(x).wait_send()
        to_core(x).wait_send()
        pass_on(x).wait_send()


def rs_scratch(lead, width):
    return [
        pltpu.VMEM(lead + (2, 4, 64, width), F32),
        pltpu.VMEM(lead + (2, 4, 64, width), BF16),
        pltpu.VMEM(lead + (2, 3, 64, width), BF16),
        pltpu.VMEM(lead + (2, 4, 16, width), F32),
        pltpu.VMEM(lead + (2, 4, 16, width), BF16),
        pltpu.VMEM(lead + (2, 3, 16, width), BF16),
        pltpu.VMEM(lead + (2, 2, 8, width), F32),
        pltpu.VMEM(lead + (2, 8, width), F32),
    ]


def per_device(held_modes, new_modes):
    own = jnp.concatenate(
        [
            held_modes.transpose(2, 0, 1, 3, 4).reshape(PLANES, HELD, DEPTH),
            new_modes.transpose(2, 0, 1, 3, 4).reshape(PLANES, NEW, DEPTH),
        ],
        1,
    )
    vmem = pl.BlockSpec(memory_space=pltpu.VMEM)
    dma = pltpu.SemaphoreType.DMA
    out_a, out_w, out_q = pl.pallas_call(
        kernel,
        out_shape=(
            jax.ShapeDtypeStruct((8, 2 * ACOLS), F32),
            jax.ShapeDtypeStruct((8, 2 * HCOLS), F32),
            jax.ShapeDtypeStruct((8, 2 * HCOLS), F32),
        ),
        in_specs=[vmem],
        out_specs=(vmem, vmem, vmem),
        scratch_shapes=[
            pltpu.VMEM((2, ROWS, DEPTH), BF16),
            pltpu.VMEM((PLANES, TOTAL, DEPTH), BF16),
            pltpu.VMEM((PLANES, NEWS, DEPTH), BF16),
            pltpu.VMEM((PLANES, 9, LINES, ROWS, LANES), F32),
            pltpu.VMEM((2 * HCOLS, DEPTH), BF16),
            pltpu.VMEM((2 * HCOLS, DEPTH), BF16),
            pltpu.VMEM((2, TOTAL, 2 * HCOLS), F32),
            pltpu.VMEM((2, TOTAL, ACOLS), F32),
            *rs_scratch((2,), HCOLS),
            *rs_scratch((), ACOLS),
            dma((2,)),
            dma((2,)),
            dma((3, PLANES)),
            dma((3, PLANES)),
            dma((PLANES,)),
            dma((3, 2, 3)),
            dma((3, 2, 3)),
            dma((3, 2, 3)),
            dma((3, 2, 3)),
            dma((3, 2)),
            dma((3, 2)),
        ],
        compiler_params=pltpu.CompilerParams(
            collective_id=0, has_side_effects=True, vmem_limit_bytes=60 * 2**20
        ),
        cost_estimate=pl.CostEstimate(
            flops=2 * 5632 * TOTAL * PLANES * DEPTH, bytes_accessed=2**20, transcendentals=0
        ),
    )(own)
    by_mode = out_a.reshape(8, NEW, 4, ROWS)
    new_third = jnp.concatenate(
        [by_mode[..., :HELD].reshape(8, NEW, 4 * HELD), by_mode[..., HELD:].reshape(8, NEW, NEWS)], 2
    ).reshape(8, 2 * ACOLS)
    return (new_third, out_w, out_q[:7])


def solution(mesh):
    placed = (P("mode", None, "grid", None, None), P("mode", None, "grid", None, None))
    return jax.shard_map(
        per_device,
        mesh=mesh,
        in_specs=placed,
        out_specs=(P("grid", "mode"), P("grid", "mode"), P("grid", "mode")),
        check_vma=False,
    )
```

```python
import jax
import jax.numpy as jnp
from jax import lax
from jax.experimental import pallas as pl
from jax.experimental.pallas import tpu as pltpu
from jax.sharding import PartitionSpec as P

MESH = pl.DeviceIdType.MESH
F32 = jnp.float32
BF16 = jnp.bfloat16
CHUNKS = 8
ORDER = ((1, 0), (1, 1), (2, 0), (0, 0), (3, 0), (2, 1), (0, 1), (3, 1))
SENDS = (0, 1, 3, 2, 4, 6, 7, 5)
RELAYED = (3, 4, 6, 7)
LANES = 128
PARTS = 6
DEPTH = PARTS * LANES
ROWS = 64
HELD = 56
NEW = 8
TOTAL = 256
NEWS = 32
GROUP = 28
HCOLS = GROUP * NEWS
NTILE = 64
NGROUP = 4
ACOLS = NGROUP * TOTAL
WEIGHT = 1.0 / 256.0


def row_every(g):
    i = 8 * g
    return 64 * (i // 56) + i % 56 if i < 224 else 64 * ((i - 224) // 8) + 56


def row_held(g):
    i = 7 * g
    return 64 * (i // 56) + i % 56


def kernel(
    given, out_a, out_w, out_q,
    own, relay, vall, vnew, slope, left, right, acc_h, acc_a,
    f_h, s1_h, r1_h, t1_h, s2_h, r2_h, t2_h, r3_h,
    f_a, s1_a, r1_a, t1_a, s2_a, r2_a, t2_a, r3_a,
    near_send, near_recv, far_send, far_recv, core_send, core_recv, pass_send, pass_recv,
    halo_send, halo_recv, own_sem, load_sem,
    rs1_send, rs1_recv, rs2_send, rs2_recv, rs3_send, rs3_recv,
):
    g = lax.axis_index("grid")
    m = lax.axis_index("mode")
    py, px, pz = g // 8, (g // 2) % 4, g % 2
    core = m + 1 - 2 * (m % 2)
    far = (m + 2) % 4

    def cell(y, x, z):
        return (y * 4 + x) * 2 + z

    along_x = [(cell(py, (px + d) % 4, pz), m) for d in (1, 2, 3)]
    along_y = [(cell((py + d) % 4, px, pz), m) for d in (1, 2, 3)]
    across = (cell(py, px, 1 - pz), m)
    beyond = (cell(py, px, 1 - pz), far)
    halo_to = ((g + 32 + 2 - 4 * pz) % 32, m)
    halo_from = ((g + 32 - 2 + 4 * pz) % 32, m)

    def load(t):
        x, h = ORDER[t]
        return pltpu.make_async_copy(given.at[x * 2 + h], own.at[t], load_sem.at[t])

    for t in range(CHUNKS):
        load(t).start()
    barrier = pltpu.get_barrier_semaphore()
    greeted = [(g, core), (g, far), across, beyond, halo_to, halo_from] + along_x + along_y
    for other in greeted:
        pl.semaphore_signal(barrier, inc=1, device_id=other, device_id_type=MESH)
    pl.semaphore_wait(barrier, len(greeted))

    def remote(src, dst, send, recv, device):
        return pltpu.make_async_remote_copy(
            src_ref=src, dst_ref=dst, send_sem=send, recv_sem=recv,
            device_id=device, device_id_type=MESH,
        )

    def slot(who):
        return pl.ds(pl.multiple_of(who * ROWS, ROWS), ROWS)

    def leave(t):
        if t in RELAYED:
            r = RELAYED.index(t)
            return remote(own.at[t], relay.at[r], near_send.at[t], near_recv.at[t], across)
        return remote(own.at[t], vall.at[t, :, slot(m)], near_send.at[t], near_recv.at[t], (g, far))

    def onward(t):
        r = RELAYED.index(t)
        return remote(relay.at[r], vall.at[t, :, slot(m)], far_send.at[t], far_recv.at[t], beyond)

    def to_core(t):
        return remote(own.at[t], vall.at[t, :, slot(m)], core_send.at[t], core_recv.at[t], (g, core))

    def pass_on(t):
        return remote(
            vall.at[t, :, slot(far)], vall.at[t, :, slot(far)], pass_send.at[t], pass_recv.at[t], (g, core)
        )

    def keep(t):
        return pltpu.make_async_copy(own.at[t], vall.at[t, :, slot(m)], own_sem.at[t])

    def halo(h):
        return remote(relay.at[2 * h + 1 - pz], relay.at[4 + h], halo_send.at[h], halo_recv.at[h], halo_to)

    load(SENDS[0]).wait()
    leave(SENDS[0]).start()
    for t in SENDS[1:]:
        load(t).wait()
    for t in range(CHUNKS):
        to_core(t).start()
        keep(t).start()

    def slopes(t, other, before, at_before, after, at_after):
        for a in range(3):
            here = [own[t, e * 3 + a].astype(F32) for e in range(2)]
            there = [own[other, e * 3 + a].astype(F32) for e in range(2)]
            for e in range(2):
                up = after[at_after, e * 3 + a].astype(F32)
                down = before[at_before, e * 3 + a].astype(F32)
                slope[t, a, e] = (up - down) * 0.5
                up, down = (here[1], there[1]) if e == 0 else (there[0], here[0])
                slope[t, 3 + a, e] = (up - down) * 0.5
                slope[t, 6 + a, e] = (
                    pltpu.roll(here[e], LANES - 1, 1) - pltpu.roll(here[e], 1, 1)
                ) * 0.5

    def at(x, h):
        return ORDER.index((x, h))

    def slopes_inner(x, h):
        slopes(at(x, h), at(x, 1 - h), own, at(x - 1, h), own, at(x + 1, h))

    def slopes_outer(h):
        slopes(at(0, h), at(0, 1 - h), relay, (4 + h) * (1 - pz) + (2 * h + 1) * pz, own, at(1, h))
        slopes(at(3, h), at(3, 1 - h), own, at(2, h), relay, 2 * h * (1 - pz) + (4 + h) * pz)

    def depart(s):
        if s + 2 < CHUNKS:
            leave(SENDS[s + 2]).start()

    def landed(t):
        leave(t).wait_recv()
        leave(t).wait_send()
        if t in RELAYED:
            onward(t).start()
        else:
            pass_on(t).start()
        depart(SENDS.index(t))

    def shared(t):
        onward(t).wait_recv()
        pass_on(t).start()

    def whole(t):
        keep(t).wait()
        to_core(t).wait_recv()
        pass_on(t).wait_recv()
        for j in range(PARTS):
            tops = [vall[t, j, q * ROWS + 48 : (q + 1) * ROWS, :].astype(F32)[8:16] for q in range(4)]
            vnew[t, j] = jnp.concatenate(tops, 0).astype(BF16)

    def spread(t, a, b, e, k):
        row = slope[t, b * 3 + a, e, k : k + 1, :]
        return jnp.broadcast_to(row, (16, LANES)).astype(BF16)[None]

    def lanes(a, e):
        return slice((e * 3 + a) * LANES, (e * 3 + a + 1) * LANES)

    def contract(t, block):
        return lax.dot_general(
            jnp.concatenate([vall[t, j] for j in range(PARTS)], 1), block,
            (((1,), (1,)), ((), ())), preferred_element_type=F32,
        )

    def build_held(t, half, into):
        base = half * 2 * HCOLS
        for e in range(2):
            v = [vnew[t, e * 3 + b].reshape(2, 16, LANES) for b in range(3)]
            for k in range(GROUP):
                s = [[spread(t, a, b, e, half * GROUP + k) for b in range(3)] for a in range(3)]
                at = base + k * NEWS
                for c in range(3):
                    w = v[0] * s[0][c] + v[1] * s[1][c] + v[2] * s[2][c]
                    into[at : at + NEWS, lanes(c, e)] = w.reshape(NEWS, LANES)
                at = at + HCOLS
                for c in range(3):
                    q = v[0] * s[c][0] + v[1] * s[c][1] + v[2] * s[c][2]
                    into[at : at + NEWS, lanes(c, e)] = q.reshape(NEWS, LANES)

    def build_new(t, group, into):
        for e in range(2):
            for k in range(NGROUP):
                s = [[spread(t, a, b, e, HELD + group * NGROUP + k) for b in range(3)] for a in range(3)]
                for r in range(0, TOTAL, NTILE):
                    v = [vall[t, e * 3 + b, r : r + NTILE].reshape(NTILE // 16, 16, LANES) for b in range(3)]
                    for c in range(3):
                        q = v[0] * s[c][0] + v[1] * s[c][1] + v[2] * s[c][2]
                        into[k * TOTAL + r : k * TOTAL + r + NTILE, lanes(c, e)] = q.reshape(NTILE, LANES)

    acc_h[...] = jnp.zeros_like(acc_h)
    acc_a[...] = jnp.zeros_like(acc_a)
    slopes_inner(1, 0)
    slopes_inner(1, 1)
    leave(SENDS[1]).start()
    slopes_inner(2, 0)
    slopes_inner(2, 1)
    landed(0)
    landed(1)
    whole(0)
    build_held(0, 0, left)
    build_held(0, 1, left)
    whole(1)

    def tick(t, following, now, then):
        for half in range(2):
            build_held(following, half, then)
            acc_h[half] += contract(t, now[half * 2 * HCOLS : (half + 1) * 2 * HCOLS])

    def before1():
        landed(3)
        landed(2)
        whole(2)

    def before2():
        landed(4)
        halo(0).start()
        shared(3)
        halo(0).wait_recv()
        slopes_outer(0)
        whole(3)

    def before3():
        landed(6)
        shared(4)
        landed(7)
        halo(1).start()
        whole(4)

    def before4():
        landed(5)
        shared(6)
        whole(5)

    def before5():
        halo(1).wait_recv()
        slopes_outer(1)
        shared(7)
        whole(6)

    def ticks(i, carry):
        pl.when(i == 1)(before2)
        pl.when(i == 2)(before4)
        pl.when(i == 3)(lambda: whole(7))
        tick(2 * i, 2 * i + 1, left, right)
        pl.when(i == 0)(before1)
        pl.when(i == 1)(before3)
        pl.when(i == 2)(before5)
        tick(2 * i + 1, jnp.minimum(2 * i + 2, CHUNKS - 1), right, left)
        return carry

    lax.fori_loop(0, CHUNKS // 2, ticks, 0)

    class Job:
        def __init__(self, n, bufs, width, source, maps, sinks):
            self.n, self.width, self.source, self.maps, self.sinks = n, width, source, maps, sinks
            self.f, self.s1, self.r1, self.t1, self.s2, self.r2, self.t2, self.r3 = bufs

        def first(self):
            for e in range(2):
                for p in range(4):
                    for q in range(4):
                        at = (q * 4 + p) if e == 0 else (p * 4 + q)
                        rows = [self.maps[e](2 * at + z) for z in range(2)]
                        for z in range(2):
                            self.f[e, p, q * 16 + z * 8 : q * 16 + z * 8 + 8, :] = self.source(e, rows[z])
                        self.s1[e, p, q * 16 : q * 16 + 16, :] = self.f[e, p, q * 16 : q * 16 + 16, :].astype(BF16)
            for copy in self.copies1():
                copy.start()

        def copies1(self):
            found = []
            for d in (1, 2, 3):
                for e in range(2):
                    p = ((px if e == 0 else py) + d) % 4
                    found.append(
                        remote(
                            self.s1.at[e, p], self.r1.at[e, d - 1],
                            rs1_send.at[self.n, e, d - 1], rs1_recv.at[self.n, e, d - 1],
                            (along_x if e == 0 else along_y)[d - 1],
                        )
                    )
            return found

        def second(self):
            for copy in self.copies1():
                copy.wait()
            for e in range(2):
                p = px if e == 0 else py
                t = self.f[e, p]
                for d in range(3):
                    t = t + self.r1[e, d].astype(F32)
                for q in range(4):
                    self.t1[e, q] = t[q * 16 : q * 16 + 16]
                    self.s2[e, q] = t[q * 16 : q * 16 + 16].astype(BF16)
            for copy in self.copies2():
                copy.start()

        def copies2(self):
            found = []
            for d in (1, 2, 3):
                for e in range(2):
                    q = ((py if e == 0 else px) + d) % 4
                    found.append(
                        remote(
                            self.s2.at[e, q], self.r2.at[e, d - 1],
                            rs2_send.at[self.n, e, d - 1], rs2_recv.at[self.n, e, d - 1],
                            (along_y if e == 0 else along_x)[d - 1],
                        )
                    )
            return found

        def third(self):
            for copy in self.copies2():
                copy.wait()
            for e in range(2):
                t = self.t1[e, py if e == 0 else px]
                for d in range(3):
                    t = t + self.r2[e, d].astype(F32)
                self.t2[e, 0] = t[0:8]
                self.t2[e, 1] = t[8:16]
            for copy in self.copies3():
                copy.start()

        def copies3(self):
            return [
                remote(
                    self.t2.at[e, 1 - pz], self.r3.at[e],
                    rs3_send.at[self.n, e], rs3_recv.at[self.n, e], across,
                )
                for e in range(2)
            ]

        def last(self):
            for copy in self.copies3():
                copy.wait()
            for e in range(2):
                ref, at = self.sinks[e]
                found = self.arrange((self.t2[e, pz] + self.r3[e]) * WEIGHT)
                ref[:, at : at + self.width] = found[: ref.shape[0]]

        def arrange(self, found):
            if self.n < 2:
                return found
            pieces = []
            for k in range(0, self.width, TOTAL):
                starts = range(k, k + TOTAL, ROWS)
                pieces += [found[:, i : i + HELD] for i in starts]
                pieces += [found[:, i + HELD : i + ROWS] for i in starts]
            return jnp.concatenate(pieces, 1)

    def held_job(half):
        def source(e, row):
            return acc_h[half, row : row + 8, e * HCOLS : (e + 1) * HCOLS]

        bufs = [b.at[half] for b in (f_h, s1_h, r1_h, t1_h, s2_h, r2_h, t2_h, r3_h)]
        return Job(half, bufs, HCOLS, source, (row_every, row_held),
                   ((out_w, half * HCOLS), (out_q, half * HCOLS)))

    def new_job(group):
        width = ACOLS // 2

        def source(e, row):
            return acc_a[group, row : row + 8, e * width : (e + 1) * width]

        bufs = [b.at[group] for b in (f_a, s1_a, r1_a, t1_a, s2_a, r2_a, t2_a, r3_a)]
        return Job(2 + group, bufs, width, source, (row_every, row_every),
                   ((out_a, group * ACOLS), (out_a, group * ACOLS + width)))

    jobs = [held_job(0), held_job(1), new_job(0), new_job(1)]
    jobs[0].first()
    jobs[1].first()

    one, two = left.at[0:ACOLS], right.at[0:ACOLS]

    def pairs(group):
        def pair(i, carry):
            build_new(2 * i + 1, group, two)
            acc_a[group] += contract(2 * i, one[...])
            build_new(jnp.minimum(2 * i + 2, CHUNKS - 1), group, one)
            acc_a[group] += contract(2 * i + 1, two[...])
            return carry

        build_new(0, group, one)
        lax.fori_loop(0, CHUNKS // 2, pair, 0)

    pairs(0)
    jobs[2].first()
    jobs[0].second()
    pairs(1)
    jobs[3].first()
    jobs[1].second()
    jobs[0].third()
    jobs[2].second()
    jobs[1].third()
    jobs[0].last()
    jobs[2].third()
    jobs[3].second()
    jobs[1].last()
    jobs[2].last()
    jobs[3].third()
    jobs[3].last()
    for t in range(CHUNKS):
        if t in RELAYED:
            onward(t).wait_send()
        to_core(t).wait_send()
        pass_on(t).wait_send()
    halo(0).wait_send()
    halo(1).wait_send()


def rs_scratch(lead, width):
    return [
        pltpu.VMEM(lead + (2, 4, 64, width), F32),
        pltpu.VMEM(lead + (2, 4, 64, width), BF16),
        pltpu.VMEM(lead + (2, 3, 64, width), BF16),
        pltpu.VMEM(lead + (2, 4, 16, width), F32),
        pltpu.VMEM(lead + (2, 4, 16, width), BF16),
        pltpu.VMEM(lead + (2, 3, 16, width), BF16),
        pltpu.VMEM(lead + (2, 2, 8, width), F32),
        pltpu.VMEM(lead + (2, 8, width), F32),
    ]


def per_device(held_modes, new_modes):
    own = jnp.concatenate([held_modes, new_modes], 0)
    own = own.transpose(2, 3, 1, 0, 4).reshape(CHUNKS, PARTS, ROWS, LANES)
    vmem = pl.BlockSpec(memory_space=pltpu.VMEM)
    dma = pltpu.SemaphoreType.DMA
    out_a, out_w, out_q = pl.pallas_call(
        kernel,
        out_shape=(
            jax.ShapeDtypeStruct((8, 2 * ACOLS), F32),
            jax.ShapeDtypeStruct((8, 2 * HCOLS), F32),
            jax.ShapeDtypeStruct((7, 2 * HCOLS), F32),
        ),
        in_specs=[pl.BlockSpec(memory_space=pl.ANY)],
        out_specs=(vmem, vmem, vmem),
        scratch_shapes=[
            pltpu.VMEM((CHUNKS, PARTS, ROWS, LANES), BF16),
            pltpu.VMEM((6, PARTS, ROWS, LANES), BF16),
            pltpu.VMEM((CHUNKS, PARTS, TOTAL, LANES), BF16),
            pltpu.VMEM((CHUNKS, PARTS, NEWS, LANES), BF16),
            pltpu.VMEM((CHUNKS, 9, 2, ROWS, LANES), F32),
            pltpu.VMEM((4 * HCOLS, DEPTH), BF16),
            pltpu.VMEM((4 * HCOLS, DEPTH), BF16),
            pltpu.VMEM((2, TOTAL, 2 * HCOLS), F32),
            pltpu.VMEM((2, TOTAL, ACOLS), F32),
            *rs_scratch((2,), HCOLS),
            *rs_scratch((2,), ACOLS // 2),
            *[dma((CHUNKS,))] * 8,
            dma((2,)),
            dma((2,)),
            dma((CHUNKS,)),
            dma((CHUNKS,)),
            dma((4, 2, 3)),
            dma((4, 2, 3)),
            dma((4, 2, 3)),
            dma((4, 2, 3)),
            dma((4, 2)),
            dma((4, 2)),
        ],
        compiler_params=pltpu.CompilerParams(
            collective_id=0, has_side_effects=True, vmem_limit_bytes=60 * 2**20
        ),
        cost_estimate=pl.CostEstimate(
            flops=2 * 5632 * TOTAL * CHUNKS * DEPTH, bytes_accessed=2**20, transcendentals=0
        ),
    )(own)
    return (out_a, out_w, out_q)


def solution(mesh):
    placed = (P("mode", None, "grid", None, None), P("mode", None, "grid", None, None))
    return jax.shard_map(
        per_device,
        mesh=mesh,
        in_specs=placed,
        out_specs=(P("grid", "mode"), P("grid", "mode"), P("grid", "mode")),
        check_vma=False,
    )
```

```python
import jax
import jax.numpy as jnp
from jax import lax
from jax.experimental import pallas as pl
from jax.experimental.pallas import tpu as pltpu
from jax.sharding import PartitionSpec as P

MESH = pl.DeviceIdType.MESH
F32 = jnp.float32
BF16 = jnp.bfloat16
CHUNKS = 8
ORDER = ((1, 0), (1, 1), (2, 0), (0, 0), (3, 0), (2, 1), (0, 1), (3, 1))
SENDS = (0, 1, 3, 2, 4, 6, 7, 5)
RELAYED = (3, 4, 6, 7)
LANES = 128
PARTS = 6
DEPTH = PARTS * LANES
ROWS = 64
HELD = 56
NEW = 8
TOTAL = 256
NEWS = 32
GROUP = 28
HCOLS = GROUP * NEWS
NTILE = 64
NGROUP = 4
ACOLS = NGROUP * TOTAL
WEIGHT = 1.0 / 256.0


def row_every(g):
    i = 8 * g
    return 64 * (i // 56) + i % 56 if i < 224 else 64 * ((i - 224) // 8) + 56


def row_held(g):
    i = 7 * g
    return 64 * (i // 56) + i % 56


def kernel(
    given, out_a, out_w, out_q,
    own, relay, vall, vnew, slope, left, right, acc_h, acc_a,
    f_h, s1_h, r1_h, t1_h, s2_h, r2_h, t2_h, r3_h,
    f_a, s1_a, r1_a, t1_a, s2_a, r2_a, t2_a, r3_a,
    near_send, near_recv, far_send, far_recv, core_send, core_recv, pass_send, pass_recv,
    halo_send, halo_recv, own_sem, load_sem,
    rs1_send, rs1_recv, rs2_send, rs2_recv, rs3_send, rs3_recv,
):
    g = lax.axis_index("grid")
    m = lax.axis_index("mode")
    py, px, pz = g // 8, (g // 2) % 4, g % 2
    core = m + 1 - 2 * (m % 2)
    far = (m + 2) % 4

    def cell(y, x, z):
        return (y * 4 + x) * 2 + z

    along_x = [(cell(py, (px + d) % 4, pz), m) for d in (1, 2, 3)]
    along_y = [(cell((py + d) % 4, px, pz), m) for d in (1, 2, 3)]
    across = (cell(py, px, 1 - pz), m)
    beyond = (cell(py, px, 1 - pz), far)
    halo_to = ((g + 32 + 2 - 4 * pz) % 32, m)
    halo_from = ((g + 32 - 2 + 4 * pz) % 32, m)

    def load(t):
        x, h = ORDER[t]
        return pltpu.make_async_copy(given.at[x * 2 + h], own.at[t], load_sem.at[t])

    for t in range(CHUNKS):
        load(t).start()
    barrier = pltpu.get_barrier_semaphore()
    greeted = [(g, core), (g, far), across, beyond, halo_to, halo_from] + along_x + along_y
    for other in greeted:
        pl.semaphore_signal(barrier, inc=1, device_id=other, device_id_type=MESH)
    pl.semaphore_wait(barrier, len(greeted))

    def remote(src, dst, send, recv, device):
        return pltpu.make_async_remote_copy(
            src_ref=src, dst_ref=dst, send_sem=send, recv_sem=recv,
            device_id=device, device_id_type=MESH,
        )

    def slot(who):
        return pl.ds(pl.multiple_of(who * ROWS, ROWS), ROWS)

    def leave(t):
        if t in RELAYED:
            r = RELAYED.index(t)
            return remote(own.at[t], relay.at[r], near_send.at[t], near_recv.at[t], across)
        return remote(own.at[t], vall.at[t, :, slot(m)], near_send.at[t], near_recv.at[t], (g, far))

    def onward(t):
        r = RELAYED.index(t)
        return remote(relay.at[r], vall.at[t, :, slot(m)], far_send.at[t], far_recv.at[t], beyond)

    def to_core(t):
        return remote(own.at[t], vall.at[t, :, slot(m)], core_send.at[t], core_recv.at[t], (g, core))

    def pass_on(t):
        return remote(
            vall.at[t, :, slot(far)], vall.at[t, :, slot(far)], pass_send.at[t], pass_recv.at[t], (g, core)
        )

    def keep(t):
        return pltpu.make_async_copy(own.at[t], vall.at[t, :, slot(m)], own_sem.at[t])

    def halo(h):
        return remote(relay.at[2 * h + 1 - pz], relay.at[4 + h], halo_send.at[h], halo_recv.at[h], halo_to)

    load(SENDS[0]).wait()
    leave(SENDS[0]).start()
    for t in SENDS[1:]:
        load(t).wait()
    for t in range(CHUNKS):
        to_core(t).start()
        keep(t).start()

    def slopes(t, other, before, at_before, after, at_after):
        for a in range(3):
            here = [own[t, e * 3 + a].astype(F32) for e in range(2)]
            there = [own[other, e * 3 + a].astype(F32) for e in range(2)]
            for e in range(2):
                up = after[at_after, e * 3 + a].astype(F32)
                down = before[at_before, e * 3 + a].astype(F32)
                slope[t, a, e] = (up - down) * 0.5
                up, down = (here[1], there[1]) if e == 0 else (there[0], here[0])
                slope[t, 3 + a, e] = (up - down) * 0.5
                slope[t, 6 + a, e] = (
                    pltpu.roll(here[e], LANES - 1, 1) - pltpu.roll(here[e], 1, 1)
                ) * 0.5

    def at(x, h):
        return ORDER.index((x, h))

    def slopes_inner(x, h):
        slopes(at(x, h), at(x, 1 - h), own, at(x - 1, h), own, at(x + 1, h))

    def slopes_outer(h):
        slopes(at(0, h), at(0, 1 - h), relay, (4 + h) * (1 - pz) + (2 * h + 1) * pz, own, at(1, h))
        slopes(at(3, h), at(3, 1 - h), own, at(2, h), relay, 2 * h * (1 - pz) + (4 + h) * pz)

    def depart(s):
        if s + 2 < CHUNKS:
            leave(SENDS[s + 2]).start()

    def landed(t):
        leave(t).wait_recv()
        leave(t).wait_send()
        if t in RELAYED:
            onward(t).start()
        else:
            pass_on(t).start()
        depart(SENDS.index(t))

    def shared(t):
        onward(t).wait_recv()
        pass_on(t).start()

    def whole(t):
        keep(t).wait()
        to_core(t).wait_recv()
        pass_on(t).wait_recv()
        for j in range(PARTS):
            tops = [vall[t, j, q * ROWS + 48 : (q + 1) * ROWS, :].astype(F32)[8:16] for q in range(4)]
            vnew[t, j] = jnp.concatenate(tops, 0).astype(BF16)

    def spread(t, a, b, e, k):
        row = slope[t, b * 3 + a, e, k : k + 1, :]
        return jnp.broadcast_to(row, (16, LANES)).astype(BF16)[None]

    def lanes(a, e):
        return slice((e * 3 + a) * LANES, (e * 3 + a + 1) * LANES)

    def contract(t, block):
        return lax.dot_general(
            jnp.concatenate([vall[t, j] for j in range(PARTS)], 1), block,
            (((1,), (1,)), ((), ())), preferred_element_type=F32,
        )

    def build_held(t, half, into):
        base = half * 2 * HCOLS
        for e in range(2):
            v = [vnew[t, e * 3 + b].reshape(2, 16, LANES) for b in range(3)]
            for k in range(GROUP):
                s = [[spread(t, a, b, e, half * GROUP + k) for b in range(3)] for a in range(3)]
                at = base + k * NEWS
                for c in range(3):
                    w = v[0] * s[0][c] + v[1] * s[1][c] + v[2] * s[2][c]
                    into[at : at + NEWS, lanes(c, e)] = w.reshape(NEWS, LANES)
                at = at + HCOLS
                for c in range(3):
                    q = v[0] * s[c][0] + v[1] * s[c][1] + v[2] * s[c][2]
                    into[at : at + NEWS, lanes(c, e)] = q.reshape(NEWS, LANES)

    def build_new(t, group, into):
        for e in range(2):
            for k in range(NGROUP):
                s = [[spread(t, a, b, e, HELD + group * NGROUP + k) for b in range(3)] for a in range(3)]
                for r in range(0, TOTAL, NTILE):
                    v = [vall[t, e * 3 + b, r : r + NTILE].reshape(NTILE // 16, 16, LANES) for b in range(3)]
                    for c in range(3):
                        q = v[0] * s[c][0] + v[1] * s[c][1] + v[2] * s[c][2]
                        into[k * TOTAL + r : k * TOTAL + r + NTILE, lanes(c, e)] = q.reshape(NTILE, LANES)

    acc_h[...] = jnp.zeros_like(acc_h)
    acc_a[...] = jnp.zeros_like(acc_a)
    slopes_inner(1, 0)
    slopes_inner(1, 1)
    leave(SENDS[1]).start()
    slopes_inner(2, 0)
    slopes_inner(2, 1)
    landed(0)
    landed(1)
    whole(0)
    build_held(0, 0, left)
    build_held(0, 1, left)
    whole(1)

    def tick(t, following, now, then):
        for half in range(2):
            build_held(following, half, then)
            acc_h[half] += contract(t, now[half * 2 * HCOLS : (half + 1) * 2 * HCOLS])

    def before1():
        landed(3)
        landed(2)
        whole(2)

    def before2():
        landed(4)
        halo(0).start()
        shared(3)
        halo(0).wait_recv()
        slopes_outer(0)
        whole(3)

    def before3():
        landed(6)
        shared(4)
        landed(7)
        halo(1).start()
        whole(4)

    def before4():
        landed(5)
        shared(6)
        whole(5)

    def before5():
        halo(1).wait_recv()
        slopes_outer(1)
        shared(7)
        whole(6)

    def ticks(i, carry):
        pl.when(i == 1)(before2)
        pl.when(i == 2)(before4)
        pl.when(i == 3)(lambda: whole(7))
        tick(2 * i, 2 * i + 1, left, right)
        pl.when(i == 0)(before1)
        pl.when(i == 1)(before3)
        pl.when(i == 2)(before5)
        tick(2 * i + 1, jnp.minimum(2 * i + 2, CHUNKS - 1), right, left)
        return carry

    lax.fori_loop(0, CHUNKS // 2, ticks, 0)

    class Job:
        def __init__(self, n, bufs, width, source, maps, sinks):
            self.n, self.width, self.source, self.maps, self.sinks = n, width, source, maps, sinks
            self.f, self.s1, self.r1, self.t1, self.s2, self.r2, self.t2, self.r3 = bufs

        def first(self):
            for e in range(2):
                for p in range(4):
                    for q in range(4):
                        at = (q * 4 + p) if e == 0 else (p * 4 + q)
                        rows = [self.maps[e](2 * at + z) for z in range(2)]
                        for z in range(2):
                            self.f[e, p, q * 16 + z * 8 : q * 16 + z * 8 + 8, :] = self.source(e, rows[z])
                        self.s1[e, p, q * 16 : q * 16 + 16, :] = self.f[e, p, q * 16 : q * 16 + 16, :].astype(BF16)
            for copy in self.copies1():
                copy.start()

        def copies1(self):
            found = []
            for d in (1, 2, 3):
                for e in range(2):
                    p = ((px if e == 0 else py) + d) % 4
                    found.append(
                        remote(
                            self.s1.at[e, p], self.r1.at[e, d - 1],
                            rs1_send.at[self.n, e, d - 1], rs1_recv.at[self.n, e, d - 1],
                            (along_x if e == 0 else along_y)[d - 1],
                        )
                    )
            return found

        def second(self):
            for copy in self.copies1():
                copy.wait()
            for e in range(2):
                p = px if e == 0 else py
                t = self.f[e, p]
                for d in range(3):
                    t = t + self.r1[e, d].astype(F32)
                for q in range(4):
                    self.t1[e, q] = t[q * 16 : q * 16 + 16]
                    self.s2[e, q] = t[q * 16 : q * 16 + 16].astype(BF16)
            for copy in self.copies2():
                copy.start()

        def copies2(self):
            found = []
            for d in (1, 2, 3):
                for e in range(2):
                    q = ((py if e == 0 else px) + d) % 4
                    found.append(
                        remote(
                            self.s2.at[e, q], self.r2.at[e, d - 1],
                            rs2_send.at[self.n, e, d - 1], rs2_recv.at[self.n, e, d - 1],
                            (along_y if e == 0 else along_x)[d - 1],
                        )
                    )
            return found

        def third(self):
            for copy in self.copies2():
                copy.wait()
            for e in range(2):
                t = self.t1[e, py if e == 0 else px]
                for d in range(3):
                    t = t + self.r2[e, d].astype(F32)
                self.t2[e, 0] = t[0:8]
                self.t2[e, 1] = t[8:16]
            for copy in self.copies3():
                copy.start()

        def copies3(self):
            return [
                remote(
                    self.t2.at[e, 1 - pz], self.r3.at[e],
                    rs3_send.at[self.n, e], rs3_recv.at[self.n, e], across,
                )
                for e in range(2)
            ]

        def last(self):
            for copy in self.copies3():
                copy.wait()
            for e in range(2):
                ref, at = self.sinks[e]
                found = self.arrange(self.t2[e, pz] + self.r3[e])
                ref[:, at : at + self.width] = found

        def arrange(self, found):
            if self.n < 2:
                return found
            pieces = []
            for k in range(0, self.width, TOTAL):
                starts = range(k, k + TOTAL, ROWS)
                pieces += [found[:, i : i + HELD] for i in starts]
                pieces += [found[:, i + HELD : i + ROWS] for i in starts]
            return jnp.concatenate(pieces, 1)

    def held_job(half):
        def source(e, row):
            return acc_h[half, row : row + 8, e * HCOLS : (e + 1) * HCOLS]

        bufs = [b.at[half] for b in (f_h, s1_h, r1_h, t1_h, s2_h, r2_h, t2_h, r3_h)]
        return Job(half, bufs, HCOLS, source, (row_every, row_held),
                   ((out_w, half * HCOLS), (out_q, half * HCOLS)))

    def new_job(group):
        width = ACOLS // 2

        def source(e, row):
            return acc_a[group, row : row + 8, e * width : (e + 1) * width]

        bufs = [b.at[group] for b in (f_a, s1_a, r1_a, t1_a, s2_a, r2_a, t2_a, r3_a)]
        return Job(2 + group, bufs, width, source, (row_every, row_every),
                   ((out_a, group * ACOLS), (out_a, group * ACOLS + width)))

    jobs = [held_job(0), held_job(1), new_job(0), new_job(1)]
    jobs[0].first()
    jobs[1].first()

    one, two = left.at[0:ACOLS], right.at[0:ACOLS]

    def pairs(group):
        def pair(i, carry):
            build_new(2 * i + 1, group, two)
            acc_a[group] += contract(2 * i, one[...])
            build_new(jnp.minimum(2 * i + 2, CHUNKS - 1), group, one)
            acc_a[group] += contract(2 * i + 1, two[...])
            return carry

        build_new(0, group, one)
        lax.fori_loop(0, CHUNKS // 2, pair, 0)

    pairs(0)
    jobs[2].first()
    jobs[0].second()
    pairs(1)
    jobs[3].first()
    jobs[1].second()
    jobs[0].third()
    jobs[2].second()
    jobs[1].third()
    jobs[0].last()
    jobs[2].third()
    jobs[3].second()
    jobs[1].last()
    jobs[2].last()
    jobs[3].third()
    jobs[3].last()
    for t in range(CHUNKS):
        if t in RELAYED:
            onward(t).wait_send()
        to_core(t).wait_send()
        pass_on(t).wait_send()
    halo(0).wait_send()
    halo(1).wait_send()


def rs_scratch(lead, width):
    return [
        pltpu.VMEM(lead + (2, 4, 64, width), F32),
        pltpu.VMEM(lead + (2, 4, 64, width), BF16),
        pltpu.VMEM(lead + (2, 3, 64, width), BF16),
        pltpu.VMEM(lead + (2, 4, 16, width), F32),
        pltpu.VMEM(lead + (2, 4, 16, width), BF16),
        pltpu.VMEM(lead + (2, 3, 16, width), BF16),
        pltpu.VMEM(lead + (2, 2, 8, width), F32),
        pltpu.VMEM(lead + (2, 8, width), F32),
    ]


def per_device(held_modes, new_modes):
    own = jnp.concatenate([held_modes, new_modes], 0)
    own = own.transpose(2, 3, 1, 0, 4).reshape(CHUNKS, PARTS, ROWS, LANES)
    vmem = pl.BlockSpec(memory_space=pltpu.VMEM)
    dma = pltpu.SemaphoreType.DMA
    out_a, out_w, out_q = pl.pallas_call(
        kernel,
        out_shape=(
            jax.ShapeDtypeStruct((8, 2 * ACOLS), F32),
            jax.ShapeDtypeStruct((8, 2 * HCOLS), F32),
            jax.ShapeDtypeStruct((8, 2 * HCOLS), F32),
        ),
        in_specs=[pl.BlockSpec(memory_space=pl.ANY)],
        out_specs=(vmem, vmem, vmem),
        scratch_shapes=[
            pltpu.VMEM((CHUNKS, PARTS, ROWS, LANES), BF16),
            pltpu.VMEM((6, PARTS, ROWS, LANES), BF16),
            pltpu.VMEM((CHUNKS, PARTS, TOTAL, LANES), BF16),
            pltpu.VMEM((CHUNKS, PARTS, NEWS, LANES), BF16),
            pltpu.VMEM((CHUNKS, 9, 2, ROWS, LANES), F32),
            pltpu.VMEM((4 * HCOLS, DEPTH), BF16),
            pltpu.VMEM((4 * HCOLS, DEPTH), BF16),
            pltpu.VMEM((2, TOTAL, 2 * HCOLS), F32),
            pltpu.VMEM((2, TOTAL, ACOLS), F32),
            *rs_scratch((2,), HCOLS),
            *rs_scratch((2,), ACOLS // 2),
            *[dma((CHUNKS,))] * 8,
            dma((2,)),
            dma((2,)),
            dma((CHUNKS,)),
            dma((CHUNKS,)),
            dma((4, 2, 3)),
            dma((4, 2, 3)),
            dma((4, 2, 3)),
            dma((4, 2, 3)),
            dma((4, 2)),
            dma((4, 2)),
        ],
        compiler_params=pltpu.CompilerParams(
            collective_id=0, has_side_effects=True, vmem_limit_bytes=60 * 2**20
        ),
        cost_estimate=pl.CostEstimate(
            flops=2 * 5632 * TOTAL * CHUNKS * DEPTH, bytes_accessed=2**20, transcendentals=0
        ),
    )(own)
    return (out_a * WEIGHT, out_w * WEIGHT, out_q[:7] * WEIGHT)


def solution(mesh):
    placed = (P("mode", None, "grid", None, None), P("mode", None, "grid", None, None))
    return jax.shard_map(
        per_device,
        mesh=mesh,
        in_specs=placed,
        out_specs=(P("grid", "mode"), P("grid", "mode"), P("grid", "mode")),
        check_vma=False,
    )
```
